256 devices in a mesh: row: 32 (over z, x), col: 8 (over y, core).
Axes of the slice: x: 4, y: 4, z: 8, core: 2. Of those that a mesh axis runs over, the one named last changes fastest.
Arguments:
- frontier: bfloat16 [65536, 128], P(('row', 'col')), may hold values from 0 to 8, as said below
- visited: int32 [65536, 128], P(('row', 'col')), may hold values 0 or 1
- tile_rows: int32 [32, 8, 32, 5], P('row', 'col'), may hold values from 0 to 1
- tile_cols: int32 [32, 8, 32, 5], P('row', 'col'), may hold values from 0 to 15
- tile_bits: bfloat16 [32, 8, 32, 5, 128, 128], P('row', 'col'), may hold values from 0 to 1, as said below
Outputs:
- depth_out: int32 [65536, 128], P(('row', 'col'))
- reach_out: float32 [65536, 128], P(('row', 'col'))
The draws below stay inside these ranges and needn't reach their ends.
Inputs may be any that keep to these rules, and one draw needn't show every extreme that they name: `frontier`: every entry is 0 or lies between 0.25 and 8. `tile_bits`: entries are 0 or 1.
All inputs are finite; a program needn't handle non-finite values. No bound on the sum of `visited` on one device may be relied on, other than what follows from the above.
Results may differ from the reference program's by a relative error of at most 0.0065.
Values may be sent and summed in bfloat16 or wider, within the bound.
No kernel may reach another device: no remote copies, remote signals or barrier semaphores. Data moves between devices by JAX's collectives and lax.ppermute only.
A program may use at most 64 MiB of HBM per device.

```python
import jax
import jax.numpy as jnp
from jax import lax

SOURCES = 128
TILE = 128
VERT_DEV = 256
TILES_DEV = 160
LEVELS = 4
VERTICES = 65536
SLOTS = 5
N_ROW = 32
N_COL = 8


def draw_frontier(key, part):
    key_live = jax.random.fold_in(key, 11)
    key_value = jax.random.fold_in(key, 12)
    key_order = jax.random.fold_in(key, 13)
    key_rate = jax.random.fold_in(key, 14)
    blocks = N_ROW * N_COL
    shape = (VERT_DEV * blocks, SOURCES)
    order = jax.random.permutation(key_order, SOURCES)
    dead_count = max(SOURCES // 16, 1)
    weak_count = max(SOURCES // 4, 1)
    dense_count = max(SOURCES // 4, 1)
    dead = order < dead_count
    weak = (order >= dead_count) & (order < dead_count + weak_count)
    dense = (order >= dead_count + weak_count) & (order < dead_count + weak_count + dense_count)
    rate_spread = jax.random.uniform(key_rate, (blocks, SOURCES), jnp.float32)
    block_rates = jnp.exp(jnp.log(0.03) + (jnp.log(0.5) - jnp.log(0.03)) * rate_spread)
    vertex_rates = jnp.repeat(block_rates, VERT_DEV, axis=0)
    rates = jnp.where(dense[None, :], vertex_rates, 0.003)
    live = (jax.random.uniform(key_live, shape, jnp.float32) < rates) & jnp.logical_not(dead)[None, :]
    spread = jax.random.uniform(key_value, shape, jnp.float32)
    strong_values = jnp.exp(jnp.log(0.5) + (jnp.log(4.0) - jnp.log(0.5)) * spread)
    weak_values = jnp.exp(jnp.log(0.25) + (jnp.log(0.8) - jnp.log(0.25)) * spread)
    values = jnp.where(weak[None, :], weak_values, strong_values)
    return jnp.where(live, values, 0.0).astype(jnp.float32).astype(jnp.bfloat16)


def draw_tile_bits(key, part):
    density = 16.0 * VERT_DEV / (TILES_DEV * TILE * TILE)
    shape = (N_ROW, N_COL, N_ROW, SLOTS, TILE, TILE)
    edges = jax.random.uniform(jax.random.fold_in(key, 21), shape, jnp.float32) < density
    return edges.astype(jnp.float32).astype(jnp.bfloat16)


def place_ends(entries, stream_key, smallest, top_value):
    place = [jax.random.randint(jax.random.fold_in(stream_key, axis), (), 0, length) for axis, length in enumerate(entries.shape)]
    main_axis = entries.shape.index(max(entries.shape))
    neighbour = place[:main_axis] + [(place[main_axis] + 1) % entries.shape[main_axis]] + place[main_axis + 1:]
    return entries.at[tuple(place)].set(smallest).at[tuple(neighbour)].set(top_value)


def setup_inputs(seed: int = 0) -> dict:
    splits = jax.random.split(jax.random.key(seed), 6)
    frontier = draw_frontier(jax.random.fold_in(splits[5], 71), 0)
    visited = place_ends((jax.random.randint(splits[1], (VERTICES, SOURCES), 0, 4) < 1).astype(jnp.int32), jax.random.fold_in(splits[1], 1), 0, 1)
    tile_rows = place_ends(jax.random.randint(splits[2], (N_ROW, N_COL, N_ROW, SLOTS), 0, VERT_DEV // TILE), jax.random.fold_in(splits[2], 1), 0, (VERT_DEV // TILE) - 1).astype(jnp.int32)
    tile_cols = place_ends(jax.random.randint(splits[3], (N_ROW, N_COL, N_ROW, SLOTS), 0, N_COL * VERT_DEV // TILE), jax.random.fold_in(splits[3], 1), 0, (N_COL * VERT_DEV // TILE) - 1).astype(jnp.int32)
    tile_bits = draw_tile_bits(jax.random.fold_in(splits[5], 71), 0)
    return dict(frontier=frontier, visited=visited, tile_rows=tile_rows, tile_cols=tile_cols, tile_bits=tile_bits)


def expand(current, tile_rows, tile_cols, tile_bits):
    width = current.shape[1]
    col_tiles = N_COL * VERT_DEV // TILE
    blocked = current.reshape(N_ROW, N_COL, VERT_DEV // TILE, TILE, width)

    def one_row(row_pos):
        def one_device(running, col_pos):
            source_part = lax.dynamic_index_in_dim(blocked, col_pos, 1, keepdims=False)
            row_ids = tile_rows[row_pos, col_pos]
            col_ids = tile_cols[row_pos, col_pos]
            edge_bits = tile_bits[row_pos, col_pos].astype(jnp.float32)
            picked = jnp.take_along_axis(source_part, row_ids[:, :, None, None], axis=1).astype(jnp.float32)
            products = jnp.einsum("qtkn,qtks->qtns", edge_bits, picked, precision=lax.Precision.HIGHEST)
            summed = jax.ops.segment_sum(products.reshape(-1, TILE, width), col_ids.reshape(-1).astype(jnp.int32), num_segments=col_tiles)
            rounded = lax.optimization_barrier(summed.astype(jnp.bfloat16))
            return running + rounded.astype(jnp.float32), None

        zero_sums = jnp.zeros((col_tiles, TILE, width), jnp.float32)
        running, unused = lax.scan(one_device, zero_sums, jnp.arange(N_COL, dtype=jnp.int32))
        return running

    result = lax.map(one_row, jnp.arange(N_ROW, dtype=jnp.int32))
    return result.reshape(-1, width)


def reference(frontier, visited, tile_rows, tile_cols, tile_bits):
    visited_now = (visited != 0) | (frontier > 0)
    depth_out = jnp.where(visited_now, 0, LEVELS + 1).astype(jnp.int32)
    reach_out = frontier.astype(jnp.float32)
    scaling = jnp.ones((SOURCES,), jnp.float32)
    current = frontier
    for level_step in range(1, LEVELS + 1):
        raw_sum = expand(current, tile_rows, tile_cols, tile_bits)
        newly_hit = (raw_sum > 0) & jnp.logical_not(visited_now)
        reached = jnp.where(newly_hit, raw_sum, jnp.zeros_like(raw_sum))
        counted = jnp.sum(newly_hit.astype(jnp.float32), axis=0)
        totals = jnp.sum(reached, axis=0)
        scaling = scaling / jnp.maximum(scaling * totals / jnp.maximum(counted, 1.0), 1.0)
        reach_out = reach_out + scaling[None, :] * reached
        depth_out = jnp.where(newly_hit, level_step, depth_out).astype(jnp.int32)
        visited_now = visited_now | newly_hit
        current = reached.astype(jnp.bfloat16)
    return depth_out, reach_out
```

```python
import functools

import jax
import jax.numpy as jnp
from jax import lax
from jax.experimental import pallas as pl
from jax.experimental.pallas import tpu as pltpu
from jax.sharding import Mesh
from jax.sharding import PartitionSpec as P

LEVELS = 4
COL = ("y", "core")
ROW = ("z", "x")
ROW_COL = ("z", "x", "y", "core")


def shifted(shard, axis, by):
    size = lax.axis_size(axis)
    return lax.ppermute(shard, axis, [(i, (i + by) % size) for i in range(size)])


def expand_kernel(counts, has_running, closing, block_of, row_of, dest_of, bits, *refs):
    blocks, refs = refs[: len(counts)], refs[len(counts) :]
    if has_running:
        running, refs = refs[0], refs[1:]
    out = refs[0]
    total = refs[1] if closing else out
    slots = row_of.shape[0] // 32
    if has_running:
        total[...] = running[...]
    else:
        total[...] = jnp.zeros_like(total)
    first = 0
    for block_ref, count in zip(blocks, counts):

        def one_block(number, carry, block_ref=block_ref, first=first):
            source = block_of[first + number]
            for slot in range(slots):
                place = source * slots + slot
                start = pl.multiple_of(row_of[place] * 128, 128)
                product = jnp.dot(
                    block_ref[number, :, pl.ds(start, 128)],
                    bits[place],
                    preferred_element_type=jnp.float32,
                )
                total[dest_of[place]] += product
            return carry

        lax.fori_loop(0, count, one_block, 0)
        first += count
    if closing:
        for part in range(8):
            out[part, :, :128] = total[2 * part].astype(out.dtype)
            out[part, :, 128:] = total[2 * part + 1].astype(out.dtype)


def expand(blocks, numbers, row_of, dest_of, bits, running, closing):
    counts = tuple(block.shape[0] for block in blocks)
    vmem = pl.BlockSpec(memory_space=pltpu.VMEM)
    smem = pl.BlockSpec(memory_space=pltpu.SMEM)
    operands = [*blocks] + ([running] if running is not None else [])
    shape = (
        jax.ShapeDtypeStruct((8, 128, 256), jnp.bfloat16)
        if closing
        else jax.ShapeDtypeStruct((16, 128, 128), jnp.float32)
    )
    tiles = sum(counts) * (row_of.shape[0] // 32)
    return pl.pallas_call(
        functools.partial(expand_kernel, counts, running is not None, closing),
        out_shape=shape,
        in_specs=[smem] * 3 + [vmem] * (1 + len(operands)),
        out_specs=vmem,
        scratch_shapes=[pltpu.VMEM((16, 128, 128), jnp.float32)] if closing else [],
        compiler_params=pltpu.CompilerParams(vmem_limit_bytes=24 * 2**20),
        cost_estimate=pl.CostEstimate(
            flops=tiles * 2 * 128**3, bytes_accessed=tiles * 32768, transcendentals=0
        ),
    )(jnp.concatenate(numbers), row_of, dest_of, bits, *operands)


def gathered(current):
    z, x = lax.axis_index("z"), lax.axis_index("x")

    def named(pair, first, z_from):
        return pair, (z_from % 8) * 4 + (x - first - jnp.arange(2)) % 4

    beside = [current] + [shifted(current, "x", k) for k in (1, 2, 3)]
    pairs = [jnp.stack(beside[:2]), jnp.stack(beside[2:])]
    early = [named(pair, 2 * n, z) for n, pair in enumerate(pairs)]
    late = []
    up, down = list(pairs), list(pairs)
    for k in range(1, 5):
        group = early if k < 3 else late
        for n in range(2):
            if k < 4 or n == 0:
                up[n] = shifted(up[n], "z", 1)
                group.append(named(up[n], 2 * n, z - k))
            if k < 4 or n == 1:
                down[n] = shifted(down[n], "z", -1)
                group.append(named(down[n], 2 * n, z + k))
    return early, late


def summed_to_owner(parts):
    pairs = parts[:4].astype(jnp.float32) + shifted(parts[4:], "core", 1).astype(jnp.float32)
    rounded = pairs.astype(jnp.bfloat16)
    total = rounded[0].astype(jnp.float32)
    for k in range(1, 4):
        total = total + shifted(rounded[k], "y", k).astype(jnp.float32)
    return total


def summed_everywhere(stats):
    stats = stats + shifted(stats, "core", 1)
    total = stats
    for k in range(1, 4):
        total = total + shifted(stats, "y", k)
    spread = jnp.broadcast_to(total[None], (32, *total.shape))
    return lax.all_to_all(spread, ROW, 0, 0, tiled=True).sum(axis=0)


def on_device(frontier, visited, tile_rows, tile_cols, tile_bits):
    bits = tile_bits.reshape(-1, 128, 128)
    row_of = tile_rows.reshape(-1)
    column = tile_cols.reshape(-1)
    owner, half = column // 2, column % 2
    away = ((owner // 2) - lax.axis_index("y")) % 4
    apart = (owner % 2) ^ lax.axis_index("core")
    dest_of = apart * 8 + away * 2 + half

    current = frontier.T
    seen = ((visited != 0) | (frontier > 0)).astype(jnp.float32).T > 0
    depth = jnp.where(seen, 0, LEVELS + 1)
    stats, held_all = [], []
    for level in range(1, LEVELS + 1):
        early, late = gathered(current)
        running = expand(*zip(*early), row_of, dest_of, bits, None, False)
        parts = expand(*zip(*late), row_of, dest_of, bits, running, True)
        raw = summed_to_owner(parts)
        fresh = (raw > 0) & jnp.logical_not(seen)
        held = jnp.where(fresh, raw, 0.0)
        stats += [fresh.astype(jnp.float32).sum(axis=1), held.sum(axis=1)]
        depth = jnp.where(fresh, level, depth)
        seen = seen | fresh
        current = held.astype(jnp.bfloat16)
        held_all.append(held)
    sums = summed_everywhere(jnp.stack(stats))
    scaling = jnp.ones_like(sums[0])
    reach = frontier.astype(jnp.float32)
    for level in range(LEVELS):
        count, total = sums[2 * level], sums[2 * level + 1]
        scaling = scaling / jnp.maximum(scaling * total / jnp.maximum(count, 1.0), 1.0)
        reach = reach + scaling[None, :] * held_all[level].T
    return depth.T.astype(jnp.int32), reach


def solution(mesh):
    torus = Mesh(mesh.devices.reshape(8, 4, 4, 2), ROW_COL)
    placed = (
        P(ROW_COL, None),
        P(ROW_COL, None),
        P(ROW, COL, None, None),
        P(ROW, COL, None, None),
        P(ROW, COL, None, None, None, None),
    )
    return jax.shard_map(
        on_device,
        mesh=torus,
        in_specs=placed,
        out_specs=(P(ROW_COL, None), P(ROW_COL, None)),
        check_vma=False,
    )
```

```python
import functools

import jax
import jax.numpy as jnp
from jax import lax
from jax.experimental import pallas as pl
from jax.experimental.pallas import tpu as pltpu
from jax.sharding import Mesh
from jax.sharding import PartitionSpec as P

LEVELS = 4
COL = ("y", "core")
ROW = ("z", "x")
ROW_COL = ("z", "x", "y", "core")


def shifted(shard, axis, by):
    size = lax.axis_size(axis)
    return lax.ppermute(shard, axis, [(i, (i + by) % size) for i in range(size)])


def expand_kernel(counts, has_running, closing, block_of, row_of, dest_of, bits, *refs):
    blocks, refs = refs[: len(counts)], refs[len(counts) :]
    total = refs[-1]
    slots = row_of.shape[0] // 32
    if not has_running:
        total[...] = jnp.zeros_like(total)
    first = 0
    for block_ref, count in zip(blocks, counts):
        for number in range(count):
            source = block_of[first + number]
            for slot in range(slots):
                place = source * slots + slot
                start = pl.multiple_of(row_of[place] * 128, 128)
                total[dest_of[place]] += jnp.dot(
                    block_ref[number, :, pl.ds(start, 128)],
                    bits[place],
                    preferred_element_type=jnp.float32,
                )
        first += count
    if closing:
        out = refs[-2]
        for part in range(8):
            out[part, :, :128] = total[2 * part].astype(out.dtype)
            out[part, :, 128:] = total[2 * part + 1].astype(out.dtype)


def expand(group, row_of, dest_of, bits, running=None, closing=False):
    blocks, numbers = zip(*group)
    counts = tuple(block.shape[0] for block in blocks)
    vmem = pl.BlockSpec(memory_space=pltpu.VMEM)
    smem = pl.BlockSpec(memory_space=pltpu.SMEM)
    operands = [bits, *blocks] + ([] if running is None else [running])
    shapes = [jax.ShapeDtypeStruct((16, 128, 128), jnp.float32)]
    if closing:
        shapes.insert(0, jax.ShapeDtypeStruct((8, 128, 256), jnp.bfloat16))
    aliases = {} if running is None else {2 + len(operands): len(shapes) - 1}
    tiles = sum(counts) * (row_of.shape[0] // 32)
    return pl.pallas_call(
        functools.partial(expand_kernel, counts, running is not None, closing),
        out_shape=shapes,
        in_specs=[smem] * 3 + [vmem] * len(operands),
        out_specs=[vmem] * len(shapes),
        input_output_aliases=aliases,
        compiler_params=pltpu.CompilerParams(vmem_limit_bytes=4 * 2**20),
        cost_estimate=pl.CostEstimate(
            flops=tiles * 2 * 128**3, bytes_accessed=tiles * 32768, transcendentals=0
        ),
    )(jnp.concatenate(numbers), row_of, dest_of, *operands)[0]


def expanded(current, row_of, dest_of, bits):
    z, x = lax.axis_index("z"), lax.axis_index("x")

    def named(pair, first, z_from):
        return pair, (z_from % 8) * 4 + (x - first - jnp.arange(2)) % 4

    beside = [current] + [shifted(current, "x", k) for k in (1, 2, 3)]
    pairs = [jnp.stack(beside[:2]), jnp.stack(beside[2:])]
    group = [named(pair, 2 * n, z) for n, pair in enumerate(pairs)]
    up, down = list(pairs), list(pairs)
    for k in range(1, 5):
        if k == 4:
            running, up, down = lax.optimization_barrier((running, up, down))
        for n in range(2):
            if k < 4 or n == 0:
                up[n] = shifted(up[n], "z", 1)
                group.append(named(up[n], 2 * n, z - k))
            if k < 4 or n == 1:
                down[n] = shifted(down[n], "z", -1)
                group.append(named(down[n], 2 * n, z + k))
        if k == 2:
            running = expand(group, row_of, dest_of, bits)
            group = []
    return expand(group, row_of, dest_of, bits, running, True)


def summed_to_owner(parts):
    pairs = parts[:4].astype(jnp.float32) + shifted(parts[4:], "core", 1).astype(jnp.float32)
    rounded = pairs.astype(jnp.bfloat16)
    total = rounded[0].astype(jnp.float32)
    for k in range(1, 4):
        total = total + shifted(rounded[k], "y", k).astype(jnp.float32)
    return total


def summed_everywhere(stats):
    stats = stats + shifted(stats, "core", 1)
    total = stats
    for k in range(1, 4):
        total = total + shifted(stats, "y", k)
    spread = jnp.broadcast_to(total[None], (32, *total.shape))
    return lax.all_to_all(spread, ROW, 0, 0, tiled=True).sum(axis=0)


def on_device(frontier, visited, tile_rows, tile_cols, tile_bits):
    bits = tile_bits.reshape(-1, 128, 128)
    row_of = tile_rows.reshape(-1)
    column = tile_cols.reshape(-1)
    owner, half = column // 2, column % 2
    away = ((owner // 2) - lax.axis_index("y")) % 4
    apart = (owner % 2) ^ lax.axis_index("core")
    dest_of = apart * 8 + away * 2 + half

    current = frontier.T
    seen = ((visited != 0) | (frontier > 0)).astype(jnp.float32).T > 0
    depth = jnp.where(seen, 0, LEVELS + 1)
    stats, held_all = [], []
    for level in range(1, LEVELS + 1):
        parts = expanded(current, row_of, dest_of, bits)
        raw = summed_to_owner(parts)
        fresh = (raw > 0) & jnp.logical_not(seen)
        held = jnp.where(fresh, raw, 0.0)
        stats += [fresh.astype(jnp.float32).sum(axis=1), held.sum(axis=1)]
        depth = jnp.where(fresh, level, depth)
        seen = seen | fresh
        current = held.astype(jnp.bfloat16)
        held_all.append(lax.optimization_barrier(held.T))
    sums = summed_everywhere(jnp.stack(stats))
    scaling = jnp.ones_like(sums[0])
    reach = frontier.astype(jnp.float32)
    for level in range(LEVELS):
        count, total = sums[2 * level], sums[2 * level + 1]
        scaling = scaling / jnp.maximum(scaling * total / jnp.maximum(count, 1.0), 1.0)
        reach = reach + scaling[None, :] * held_all[level]
    return depth.T.astype(jnp.int32), reach


def solution(mesh):
    torus = Mesh(mesh.devices.reshape(8, 4, 4, 2), ROW_COL)
    placed = (
        P(ROW_COL, None),
        P(ROW_COL, None),
        P(ROW, COL, None, None),
        P(ROW, COL, None, None),
        P(ROW, COL, None, None, None, None),
    )
    return jax.shard_map(
        on_device,
        mesh=torus,
        in_specs=placed,
        out_specs=(P(ROW_COL, None), P(ROW_COL, None)),
        check_vma=False,
    )
```

```python
import functools

import jax
import jax.numpy as jnp
from jax import lax
from jax.experimental import pallas as pl
from jax.experimental.pallas import tpu as pltpu
from jax.sharding import Mesh
from jax.sharding import PartitionSpec as P

LEVELS = 4
COL = ("y", "core")
ROW = ("z", "x")
ROW_COL = ("z", "x", "y", "core")


def shifted(shard, axis, by):
    size = lax.axis_size(axis)
    return lax.ppermute(shard, axis, [(i, (i + by) % size) for i in range(size)])


def expand_kernel(counts, has_running, closing, block_of, row_of, dest_of, bits, *refs):
    blocks, refs = refs[: len(counts)], refs[len(counts) :]
    total = refs[-1]
    slots = row_of.shape[0] // 32
    if not has_running:
        total[...] = jnp.zeros_like(total)
    first = 0
    for block_ref, count in zip(blocks, counts):
        for number in range(count):
            source = block_of[first + number]
            for slot in range(slots):
                place = source * slots + slot
                start = pl.multiple_of(row_of[place] * 128, 128)
                total[dest_of[place]] += jnp.dot(
                    block_ref[number, :, pl.ds(start, 128)],
                    bits[place],
                    preferred_element_type=jnp.float32,
                )
        first += count
    if closing:
        out = refs[-2]
        for part in range(8):
            out[part, :, :128] = total[2 * part].astype(out.dtype)
            out[part, :, 128:] = total[2 * part + 1].astype(out.dtype)


def expand(group, row_of, dest_of, bits, running=None, closing=False):
    blocks, numbers = zip(*group)
    counts = tuple(block.shape[0] for block in blocks)
    vmem = pl.BlockSpec(memory_space=pltpu.VMEM)
    smem = pl.BlockSpec(memory_space=pltpu.SMEM)
    operands = [bits, *blocks] + ([] if running is None else [running])
    shapes = [jax.ShapeDtypeStruct((16, 128, 128), jnp.float32)]
    if closing:
        shapes.insert(0, jax.ShapeDtypeStruct((8, 128, 256), jnp.bfloat16))
    aliases = {} if running is None else {2 + len(operands): len(shapes) - 1}
    tiles = sum(counts) * (row_of.shape[0] // 32)
    return pl.pallas_call(
        functools.partial(expand_kernel, counts, running is not None, closing),
        out_shape=shapes,
        in_specs=[smem] * 3 + [vmem] * len(operands),
        out_specs=[vmem] * len(shapes),
        input_output_aliases=aliases,
        compiler_params=pltpu.CompilerParams(vmem_limit_bytes=4 * 2**20),
        cost_estimate=pl.CostEstimate(
            flops=tiles * 2 * 128**3, bytes_accessed=tiles * 32768, transcendentals=0
        ),
    )(jnp.concatenate(numbers), row_of, dest_of, *operands)[0]


def expanded(current, row_of, dest_of, bits):
    z, x = lax.axis_index("z"), lax.axis_index("x")

    def named(pair, chain, z_from):
        return pair, (z_from % 8) * 4 + (x - 2 * chain - jnp.arange(2)) % 4

    beside = [current] + [shifted(current, "x", k) for k in (1, 2, 3)]
    pairs = [jnp.stack(beside[:2]), jnp.stack(beside[2:])]
    group = [named(pair, chain, z) for chain, pair in enumerate(pairs)]
    up, down = list(pairs), list(pairs)
    for k in (1, 2, 3):
        for chain in range(2):
            if k == 3:
                if chain == 0:
                    group, first = [], group
                far = shifted(up[0], "z", 2) if chain == 0 else shifted(down[1], "z", -2)
                group.append(named(far, chain, z + 4))
            up[chain] = shifted(up[chain], "z", 1)
            down[chain] = shifted(down[chain], "z", -1)
            group.append(named(up[chain], chain, z - k))
            group.append(named(down[chain], chain, z + k))
    running = expand(first, row_of, dest_of, bits)
    return expand(group, row_of, dest_of, bits, running, True)


def summed_to_owner(parts):
    pairs = parts[:4].astype(jnp.float32) + shifted(parts[4:], "core", 1).astype(jnp.float32)
    rounded = pairs.astype(jnp.bfloat16)
    total = rounded[0].astype(jnp.float32)
    for k in (2, 1, 3):
        total = total + shifted(rounded[k], "y", k).astype(jnp.float32)
    return total


def summed_everywhere(stats):
    stats = stats + shifted(stats, "core", 1)
    total = stats
    for k in (2, 1, 3):
        total = total + shifted(stats, "y", k)
    spread = jnp.broadcast_to(total[None], (32, *total.shape))
    return lax.all_to_all(spread, ROW, 0, 0, tiled=True).sum(axis=0)


def on_device(frontier, visited, tile_rows, tile_cols, tile_bits):
    bits = tile_bits.reshape(-1, 128, 128)
    row_of = tile_rows.reshape(-1)
    column = tile_cols.reshape(-1)
    owner, half = column // 2, column % 2
    away = ((owner // 2) - lax.axis_index("y")) % 4
    apart = (owner % 2) ^ lax.axis_index("core")
    dest_of = apart * 8 + away * 2 + half

    current = frontier.T
    seen = ((visited != 0) | (frontier > 0)).astype(jnp.float32).T > 0
    depth = jnp.where(seen, 0, LEVELS + 1)
    stats, held_all = [], []
    for level in range(1, LEVELS + 1):
        parts = expanded(current, row_of, dest_of, bits)
        raw = summed_to_owner(parts)
        fresh = (raw > 0) & jnp.logical_not(seen)
        held = jnp.where(fresh, raw, 0.0)
        stats += [fresh.astype(jnp.float32).sum(axis=1), held.sum(axis=1)]
        depth = jnp.where(fresh, level, depth)
        seen = seen | fresh
        current = held.astype(jnp.bfloat16)
        held_all.append(lax.optimization_barrier(held.T))
    sums = summed_everywhere(jnp.stack(stats))
    scaling = jnp.ones_like(sums[0])
    reach = frontier.astype(jnp.float32)
    for level in range(LEVELS):
        count, total = sums[2 * level], sums[2 * level + 1]
        scaling = scaling / jnp.maximum(scaling * total / jnp.maximum(count, 1.0), 1.0)
        reach = reach + scaling[None, :] * held_all[level]
    return depth.T.astype(jnp.int32), reach


def solution(mesh):
    torus = Mesh(mesh.devices.reshape(8, 4, 4, 2), ROW_COL)
    placed = (
        P(ROW_COL, None),
        P(ROW_COL, None),
        P(ROW, COL, None, None),
        P(ROW, COL, None, None),
        P(ROW, COL, None, None, None, None),
    )
    return jax.shard_map(
        on_device,
        mesh=torus,
        in_specs=placed,
        out_specs=(P(ROW_COL, None), P(ROW_COL, None)),
        check_vma=False,
    )
```

```python
import functools

import jax
import jax.numpy as jnp
from jax import lax
from jax.experimental import pallas as pl
from jax.experimental.pallas import tpu as pltpu
from jax.sharding import Mesh
from jax.sharding import PartitionSpec as P

LEVELS = 4
COL = ("y", "core")
ROW = ("z", "x")
ROW_COL = ("z", "x", "y", "core")


def shifted(shard, axis, by):
    size = lax.axis_size(axis)
    return lax.ppermute(shard, axis, [(i, (i + by) % size) for i in range(size)])


def expand_kernel(counts, has_running, closing, block_of, row_of, dest_of, bits, *refs):
    blocks, refs = refs[: len(counts)], refs[len(counts) :]
    total = refs[-2]
    slots = row_of.shape[0] // 32
    if not has_running:
        total[...] = jnp.zeros_like(total)
    first = 0
    for block_ref, count in zip(blocks, counts):
        for number in range(count):
            source = block_of[first + number]
            for slot in range(slots):
                place = source * slots + slot
                start = pl.multiple_of(row_of[place] * 128, 128)
                total[dest_of[place]] += jnp.dot(
                    block_ref[number, :, pl.ds(start, 128)],
                    bits[place],
                    preferred_element_type=jnp.float32,
                )
        first += count
    if closing:
        out = refs[-3]
        for part in range(8):
            out[part, :, :128] = total[2 * part].astype(out.dtype)
            out[part, :, 128:] = total[2 * part + 1].astype(out.dtype)


def expand(group, row_of, dest_of, bits, running=None, closing=False):
    blocks, numbers = zip(*group)
    counts = tuple(block.shape[0] for block in blocks)
    vmem = pl.BlockSpec(memory_space=pltpu.VMEM)
    smem = pl.BlockSpec(memory_space=pltpu.SMEM)
    operands = [bits, *blocks] + ([] if running is None else [running])
    shapes = [jax.ShapeDtypeStruct((16, 128, 128), jnp.float32)]
    if closing:
        shapes.insert(0, jax.ShapeDtypeStruct((8, 128, 256), jnp.bfloat16))
    aliases = {} if running is None else {2 + len(operands): len(shapes) - 1}
    aliases[3] = len(shapes)
    shapes.append(jax.ShapeDtypeStruct(bits.shape, bits.dtype))
    tiles = sum(counts) * (row_of.shape[0] // 32)
    return pl.pallas_call(
        functools.partial(expand_kernel, counts, running is not None, closing),
        out_shape=shapes,
        in_specs=[smem] * 3 + [vmem] * len(operands),
        out_specs=[vmem] * len(shapes),
        input_output_aliases=aliases,
        compiler_params=pltpu.CompilerParams(vmem_limit_bytes=4 * 2**20),
        cost_estimate=pl.CostEstimate(
            flops=tiles * 2 * 128**3, bytes_accessed=tiles * 32768, transcendentals=0
        ),
    )(jnp.concatenate(numbers), row_of, dest_of, *operands)


def expanded(current, row_of, dest_of, bits):
    z, x = lax.axis_index("z"), lax.axis_index("x")

    def named(pair, chain, z_from):
        return pair, (z_from % 8) * 4 + (x - 2 * chain - jnp.arange(2)) % 4

    beside = [current] + [shifted(current, "x", k) for k in (1, 2, 3)]
    pairs = [jnp.stack(beside[:2]), jnp.stack(beside[2:])]
    group = [named(pair, chain, z) for chain, pair in enumerate(pairs)]
    up, down = list(pairs), list(pairs)
    for k in (1, 2, 3):
        for chain in range(2):
            if k == 3:
                if chain == 0:
                    group, first = [], group
                far = shifted(up[0], "z", 2) if chain == 0 else shifted(down[1], "z", -2)
                group.append(named(far, chain, z + 4))
            up[chain] = shifted(up[chain], "z", 1)
            down[chain] = shifted(down[chain], "z", -1)
            group.append(named(up[chain], chain, z - k))
            group.append(named(down[chain], chain, z + k))
    running, bits = expand(first, row_of, dest_of, bits)
    parts, _, bits = expand(group, row_of, dest_of, bits, running, True)
    return parts, bits


def summed_to_owner(parts):
    pairs = parts[:4].astype(jnp.float32) + shifted(parts[4:], "core", 1).astype(jnp.float32)
    rounded = pairs.astype(jnp.bfloat16)
    total = rounded[0].astype(jnp.float32)
    for k in (2, 1, 3):
        total = total + shifted(rounded[k], "y", k).astype(jnp.float32)
    return total


def summed_everywhere(stats):
    stats = stats + shifted(stats, "core", 1)
    total = stats
    for k in (2, 1, 3):
        total = total + shifted(stats, "y", k)
    spread = jnp.broadcast_to(total[None], (32, *total.shape))
    return lax.all_to_all(spread, ROW, 0, 0, tiled=True).sum(axis=0)


def on_device(frontier, visited, tile_rows, tile_cols, tile_bits):
    bits = tile_bits.reshape(-1, 128, 128)
    row_of = tile_rows.reshape(-1)
    column = tile_cols.reshape(-1)
    owner, half = column // 2, column % 2
    away = ((owner // 2) - lax.axis_index("y")) % 4
    apart = (owner % 2) ^ lax.axis_index("core")
    dest_of = apart * 8 + away * 2 + half

    current = frontier.T
    seen = ((visited != 0) | (frontier > 0)).astype(jnp.float32).T > 0
    depth = jnp.where(seen, 0, LEVELS + 1)
    stats, held_all = [], []
    for level in range(1, LEVELS + 1):
        parts, bits = expanded(current, row_of, dest_of, bits)
        raw = summed_to_owner(parts)
        fresh = (raw > 0) & jnp.logical_not(seen)
        held = jnp.where(fresh, raw, 0.0)
        stats += [fresh.astype(jnp.float32).sum(axis=1), held.sum(axis=1)]
        depth = jnp.where(fresh, level, depth)
        seen = seen | fresh
        current = held.astype(jnp.bfloat16)
        held_all.append(lax.optimization_barrier(held.T))
    sums = summed_everywhere(jnp.stack(stats))
    scaling = jnp.ones_like(sums[0])
    reach = frontier.astype(jnp.float32)
    for level in range(LEVELS):
        count, total = sums[2 * level], sums[2 * level + 1]
        scaling = scaling / jnp.maximum(scaling * total / jnp.maximum(count, 1.0), 1.0)
        reach = reach + scaling[None, :] * held_all[level]
    return depth.T.astype(jnp.int32), reach


def solution(mesh):
    torus = Mesh(mesh.devices.reshape(8, 4, 4, 2), ROW_COL)
    placed = (
        P(ROW_COL, None),
        P(ROW_COL, None),
        P(ROW, COL, None, None),
        P(ROW, COL, None, None),
        P(ROW, COL, None, None, None, None),
    )
    return jax.shard_map(
        on_device,
        mesh=torus,
        in_specs=placed,
        out_specs=(P(ROW_COL, None), P(ROW_COL, None)),
        check_vma=False,
    )
```
